768 devices in a mesh: rep: 24 (over x, z_lo), fsdp: 32 (over y, z_hi, core).
Axes of the slice: x: 4, y: 8, z: 12 (z_hi: 2, z_lo: 6; z = z_hi * 6 + z_lo), core: 2. Of those that a mesh axis runs over, the one named last changes fastest.
Arguments:
- inputs: bfloat16 [147456, 4096], P(('rep', 'fsdp')), may hold values from -6 to 6
- key_grad: bfloat16 [147456, 512], P(('rep', 'fsdp')), may hold values from -16 to 16
- weights: float32 [24, 4096, 512], P('rep', 'fsdp'), may hold values from -6 to 6
- anchor: float32 [24, 4096, 512], P('rep', 'fsdp'), may hold values from -6 to 6
- adam_first: float32 [24, 4096, 512], P('rep', 'fsdp'), may hold values from -6 to 6
- adam_second: float32 [24, 4096, 512], P('rep', 'fsdp'), may hold values from 0.3 to 3
- outer_mom: float32 [24, 4096, 512], P('rep', 'fsdp'), may hold values from -6 to 6
- partner: int32 [32, 24], P('fsdp'), may hold values from 0 to 23, as said below
Outputs:
- keys: bfloat16 [147456, 512], P(('rep', 'fsdp'))
- new_anchor: float32 [24, 4096, 512], P('rep', 'fsdp')
- new_mom: float32 [24, 4096, 512], P('rep', 'fsdp')
- new_first: float32 [24, 4096, 512], P('rep', 'fsdp')
- new_second: float32 [24, 4096, 512], P('rep', 'fsdp')
The draws below stay inside these ranges and needn't reach their ends.
Inputs may be any that keep to these rules, and one draw needn't show every extreme that they name: Each row partner[s] is a matching: partner[s, partner[s, r]] = r and partner[s, r] != r for every replica r.
All inputs are finite; a program needn't handle non-finite values.
Results may differ from the reference program's by a relative error of at most 0.019.
Values may be sent and summed in bfloat16 or wider, within the bound.
No kernel may reach another device: no remote copies, remote signals or barrier semaphores. Data moves between devices by JAX's collectives and lax.ppermute only.
A program may use at most 32 MiB of HBM per device.

```python
import math
import jax
import jax.numpy as jnp
from jax import lax

D = 4096
KV = 512
TOK_DEV = 192
REPS = 24
SHARDS = 32
TOK_REP = 6144
TOKENS = 147456
DS = 128
N_FSDP = 32


def one_matching(key):
    order = jax.random.permutation(key, REPS).astype(jnp.int32)
    paired = order[jnp.arange(REPS, dtype=jnp.int32) ^ 1]
    return jnp.zeros((REPS,), jnp.int32).at[order].set(paired)


def draw_partner(key, part):
    key = jax.random.fold_in(key, 7)
    keys_all = jax.random.split(key, SHARDS)
    return jax.vmap(one_matching)(keys_all)


def levels(key, dims, cuts, low, top_value):
    gain, own = 1.0, jax.random.fold_in(key, 6)
    for position, parts in cuts:
        draws = jnp.exp(jax.random.uniform(jax.random.fold_in(own, position), (parts,), jnp.float32, low / len(cuts), top_value / len(cuts)))
        gain = gain * jnp.repeat(draws, dims[position] // parts).reshape([-1 if axis == position else 1 for axis in range(len(dims))])
    return gain


def centred(rng, extent, spread, limit, shards=(), held_as=jnp.bfloat16):
    array = jax.random.normal(rng, extent, jnp.float32) * spread
    if len(shards) > 0:
        array = levels(rng, extent, shards, -0.22, 0.18) * array
    return jnp.clip(array, min=-limit, max=limit).astype(held_as)


def setup_inputs(seed: int = 0) -> dict:
    seeds = jax.random.split(jax.random.key(seed), 9)
    inputs = centred(seeds[0], (TOKENS, D), 1.0, 6.0, ((0, 768),))
    key_grad = centred(seeds[1], (TOKENS, KV), 3.0, 16.0, ((0, 768),))
    weights = centred(seeds[2], (REPS, D, KV), 1.0, 6.0, ((0, 24), (1, 32)), jnp.float32)
    anchor = centred(seeds[3], (REPS, D, KV), 1.0, 6.0, ((0, 24), (1, 32)), jnp.float32)
    adam_first = centred(seeds[4], (REPS, D, KV), 1.0, 6.0, ((0, 24), (1, 32)), jnp.float32)
    adam_second = jnp.clip(jnp.exp(math.log(3.0) - 2.3025851 * jax.random.uniform(seeds[5], (REPS, D, KV), jnp.float32) ** levels(seeds[5], (REPS, D, KV), ((0, 24), (1, 32)), -0.2, 0.2)), 0.3, 3.0)
    outer_mom = centred(seeds[6], (REPS, D, KV), 1.0, 6.0, ((0, 24), (1, 32)), jnp.float32)
    partner = draw_partner(jax.random.fold_in(seeds[8], 71), 0)
    return dict(inputs=inputs, key_grad=key_grad, weights=weights, anchor=anchor, adam_first=adam_first, adam_second=adam_second, outer_mom=outer_mom, partner=partner)


def replica_step(packed_args):
    x_rep, dk_rep, weight, anchor_rep, first, second = packed_args
    scale = D ** (-0.5)
    packed = weight.astype(jnp.bfloat16)
    keys_rep = (jnp.dot(x_rep, packed, preferred_element_type=jnp.float32) * scale).astype(jnp.bfloat16)
    x_blocks = x_rep.reshape(N_FSDP, TOK_DEV, D)
    k_blocks = dk_rep.reshape(N_FSDP, TOK_DEV, KV)

    def add_block(carry, pair):
        x_blk, k_blk = pair
        part = lax.dot_general(x_blk, k_blk, (((0,), (0,)), ((), ())), preferred_element_type=jnp.float32) * scale
        part = lax.optimization_barrier(part.astype(jnp.bfloat16))
        return (carry + part.astype(jnp.float32), None)
    grad, _ = lax.scan(add_block, jnp.zeros((D, KV), jnp.float32), (x_blocks, k_blocks))
    first_new = 0.9 * first + 0.1 * grad
    second_new = 0.95 * second + 0.05 * grad * grad
    update = first_new / (1.0 - 0.9 ** 8) / (jnp.sqrt(second_new / (1.0 - 0.95 ** 8)) + 1e-08)
    inner = weight - 0.3 * (update + 0.1 * weight)
    delta = anchor_rep - inner
    return (keys_rep, first_new, second_new, delta)

def pair_rows(values, partner):
    blocks = values.reshape(REPS, SHARDS, DS, KV)
    index = jnp.transpose(partner.astype(jnp.int32))
    shard_ids = jnp.arange(SHARDS, dtype=jnp.int32)[None, :]
    return blocks[index, shard_ids].reshape(REPS, D, KV)

def reference(inputs, key_grad, weights, anchor, adam_first, adam_second, outer_mom, partner):
    x_all = inputs.reshape(REPS, TOK_REP, D)
    dk_all = key_grad.reshape(REPS, TOK_REP, KV)
    keys, new_first, new_second, delta = lax.map(replica_step, (x_all, dk_all, weights, anchor, adam_first, adam_second))
    delta_avg = 0.5 * (delta + pair_rows(delta, partner))
    mom_avg = 0.5 * (outer_mom + pair_rows(outer_mom, partner))
    new_mom = 0.5 * mom_avg + delta_avg
    new_anchor = anchor - 0.7 * (0.5 * new_mom + delta_avg)
    return (keys.reshape(TOKENS, KV), new_anchor, new_mom, new_first, new_second)
```

```python
import jax
import jax.numpy as jnp
from jax import lax
from jax.experimental import pallas as pl
from jax.experimental.pallas import tpu as pltpu
from jax.sharding import PartitionSpec as P

RING = 8
ORDER = (1, 3, 7, 5, 4, 2, 6, 0)
VMEM = pl.BlockSpec(memory_space=pltpu.VMEM)
HBM = pl.BlockSpec(memory_space=pl.ANY)
SMEM = pl.BlockSpec(memory_space=pltpu.SMEM)
PARAMS = pltpu.CompilerParams(vmem_limit_bytes=32 * 1024 * 1024)


def hop(move):
    pairs = []
    for y in range(RING):
        for z in range(2):
            for c in range(2):
                y2, z2, c2 = move(y, z, c)
                pairs.append(((y * 2 + z) * 2 + c, ((y2 % RING) * 2 + z2) * 2 + c2))
    return pairs


CORE = hop(lambda y, z, c: (y, z, 1 - c))
ZSWAP = hop(lambda y, z, c: (y, 1 - z, c))


def ring(step):
    return hop(lambda y, z, c: (y + step, z, c))


def send(value, pairs):
    return lax.ppermute(value, "fsdp", pairs)


def pick_kernel(table, x, k, own, other, sems):
    copies = [pltpu.make_async_copy(k, other.at[:, pl.ds(2048, 512)], sems.at[32])]
    for j in range(16):
        for half, target in ((0, own), (1, other)):
            start = pl.multiple_of(table[half * 16 + j] * 128, 128)
            copies.append(
                pltpu.make_async_copy(
                    x.at[:, pl.ds(start, 128)],
                    target.at[:, pl.ds(j * 128, 128)],
                    sems.at[half * 16 + j],
                )
            )
    for copy in copies:
        copy.start()
    for copy in copies:
        copy.wait()


def pick(inputs, key_grad, table):
    tokens = inputs.shape[0]
    return pl.pallas_call(
        pick_kernel,
        out_shape=(
            jax.ShapeDtypeStruct((tokens, 2048), jnp.bfloat16),
            jax.ShapeDtypeStruct((tokens, 2560), jnp.bfloat16),
        ),
        in_specs=[SMEM, HBM, HBM],
        out_specs=(HBM, HBM),
        scratch_shapes=[pltpu.SemaphoreType.DMA((33,))],
        compiler_params=PARAMS,
    )(table, inputs, key_grad)


def grad_kernel(scale, own, other, k, a, b, c1, c2, d2, d6, d0):
    right = jnp.concatenate([k[...], other[:, 2048:2560]], axis=0)
    places = (
        (a, 0), (a, 256), (b, 0), (b, 256), None, (d2, 0), (d6, 0), (d0, 0),
    )
    for p, place in enumerate(places):
        cols = slice(p * 256, p * 256 + 256)
        left = jnp.concatenate([own[:, cols], other[:, cols]], axis=0)
        part = scale * lax.dot_general(
            left, right, (((0,), (0,)), ((), ())), preferred_element_type=jnp.float32
        )
        if place is None:
            c1[...] = part[:128].astype(c1.dtype)
            c2[...] = part[128:].astype(c2.dtype)
        else:
            ref, row = place
            ref[row : row + 256, :] = part.astype(ref.dtype)


def grad_parts(own, other, key_grad, scale):
    bf = jnp.bfloat16
    shapes = ((512, bf), (512, bf), (128, bf), (128, bf), (256, bf), (256, bf), (256, jnp.float32))
    return pl.pallas_call(
        lambda *refs: grad_kernel(scale, *refs),
        out_shape=tuple(jax.ShapeDtypeStruct((rows, 512), kind) for rows, kind in shapes),
        in_specs=[VMEM] * 3,
        out_specs=(VMEM,) * 7,
        compiler_params=PARAMS,
        cost_estimate=pl.CostEstimate(
            flops=2 * 384 * 2048 * 512, bytes_accessed=5 << 20, transcendentals=0
        ),
    )(own, other, key_grad)


def key_kernel(scale, place, own, other, w, mine, theirs):
    y = place[0]
    total_mine = jnp.zeros(mine.shape, jnp.float32)
    total_theirs = jnp.zeros(theirs.shape, jnp.float32)
    for p, step in enumerate(ORDER):
        cols = slice(p * 256, p * 256 + 256)
        row = pl.multiple_of(lax.rem(y + step, RING) * 256, 256)
        block = w[pl.ds(row, 256), :]
        total_theirs += jnp.dot(other[:, cols], block, preferred_element_type=jnp.float32)
        total_mine += jnp.dot(own[:, cols], block, preferred_element_type=jnp.float32)
    mine[...] = scale * total_mine
    theirs[...] = (scale * total_theirs).astype(theirs.dtype)


def key_parts(place, own, other, w, scale):
    tokens = own.shape[0]
    return pl.pallas_call(
        lambda *refs: key_kernel(scale, *refs),
        out_shape=(
            jax.ShapeDtypeStruct((tokens, 512), jnp.float32),
            jax.ShapeDtypeStruct((tokens, 512), jnp.bfloat16),
        ),
        in_specs=[SMEM, VMEM, VMEM, VMEM],
        out_specs=(VMEM, VMEM),
        compiler_params=PARAMS,
        cost_estimate=pl.CostEstimate(
            flops=2 * 384 * 2048 * 512, bytes_accessed=5 << 20, transcendentals=0
        ),
    )(place, own, other, w)


def to_blocks(value, replicas):
    tiles = value.reshape(16, 8, 4, 128).transpose(0, 2, 1, 3).reshape(64, 8, 128)
    each = -(-64 // replicas)
    tiles = jnp.pad(tiles, ((0, replicas * each - 64), (0, 0), (0, 0)))
    return tiles.reshape(replicas, each * 8, 128)


def from_blocks(blocks):
    tiles = blocks.reshape(-1, 8, 128)[:64].reshape(16, 4, 8, 128)
    return tiles.transpose(0, 2, 1, 3).reshape(128, 512)


def average(value, matching):
    replicas = lax.axis_size("rep")
    blocks = to_blocks(value.astype(jnp.bfloat16), replicas)
    got = lax.all_to_all(blocks, "rep", split_axis=0, concat_axis=0, tiled=True)
    wide = got.astype(jnp.float32)
    mean = (0.5 * (wide + jnp.take(wide, matching, axis=0))).astype(jnp.bfloat16)
    back = lax.all_to_all(mean, "rep", split_axis=0, concat_axis=0, tiled=True)
    return from_blocks(back).astype(jnp.float32)


def on_device(inputs, key_grad, weights, anchor, adam_first, adam_second, outer_mom, partner):
    scale = inputs.shape[1] ** (-0.5)
    me = lax.axis_index("fsdp")
    core, zh, y = me % 2, (me // 2) % 2, me // 4
    groups = [[(r * 2 + z) * 2 + c for r in range(RING)] for z in range(2) for c in range(2)]
    matching = partner[0]
    weight = weights[0]

    steps = jnp.array(ORDER, jnp.int32)
    base = (lax.rem(y + steps, RING) * 4)[:, None] + jnp.stack([zh * 2, 2 - zh * 2])[None, :]
    base = base.reshape(16)
    table = jnp.concatenate([base + core, base + 1 - core]).astype(jnp.int32)
    own, away = pick(inputs, key_grad, table)
    other = send(away, CORE)

    packed = weight.astype(jnp.bfloat16)
    pair = jnp.concatenate([packed, send(packed, ZSWAP)], axis=0)
    gathered = lax.all_gather(pair, "fsdp", axis=0, tiled=True, axis_index_groups=groups)

    a, b, c1, c2, d2, d6, d0 = grad_parts(own, other, key_grad, scale)
    a, b = send(a, ring(1)), send(b, ring(-1))
    c1, c2 = send(c1, ring(2)), send(c2, ring(-2))
    f32 = jnp.float32
    m2 = d2.astype(f32) + a[256:].astype(f32) + jnp.pad(c1.astype(f32), ((0, 128), (0, 0)))
    m6 = d6.astype(f32) + b[256:].astype(f32) + jnp.pad(c2.astype(f32), ((128, 0), (0, 0)))
    e2 = send(m2.astype(jnp.bfloat16), ring(2))
    e6 = send(m6.astype(jnp.bfloat16), ring(-2))
    total = d0 + (a[:256].astype(f32) + b[:256].astype(f32)) + (e2.astype(f32) + e6.astype(f32))
    grad = total[:128] + send(total[128:].astype(jnp.bfloat16), ZSWAP).astype(f32)

    first_new = 0.9 * adam_first[0] + 0.1 * grad
    second_new = 0.95 * adam_second[0] + 0.05 * grad * grad
    update = first_new / (1.0 - 0.9**8) / (jnp.sqrt(second_new / (1.0 - 0.95**8)) + 1e-08)
    inner = weight - 0.3 * (update + 0.1 * weight)
    delta = anchor[0] - inner

    mom_avg = average(outer_mom[0], matching)
    delta_avg = average(delta, matching)
    mom_new = 0.5 * mom_avg + delta_avg
    anchor_new = anchor[0] - 0.7 * (0.5 * mom_new + delta_avg)

    place = jnp.reshape(y, (1,)).astype(jnp.int32)
    mine, theirs = key_parts(place, own, other, gathered, scale)
    keys = (mine + send(theirs, CORE).astype(f32)).astype(jnp.bfloat16)
    return (keys, anchor_new[None], mom_new[None], first_new[None], second_new[None])


def solution(mesh):
    shard = P("rep", "fsdp", None)
    flat = P(("rep", "fsdp"), None)
    return jax.shard_map(
        on_device,
        mesh=mesh,
        in_specs=(flat, flat, shard, shard, shard, shard, shard, P("fsdp", None)),
        out_specs=(flat, shard, shard, shard, shard),
        check_vma=False,
    )
```

```python
import jax
import jax.numpy as jnp
from jax import lax
from jax.experimental import pallas as pl
from jax.experimental.pallas import tpu as pltpu
from jax.sharding import PartitionSpec as P

RING = 8
ORDER = (1, 3, 7, 5, 4, 2, 6, 0)
VMEM = pl.BlockSpec(memory_space=pltpu.VMEM)
ANY = pl.BlockSpec(memory_space=pl.ANY)
HBM = pl.BlockSpec(memory_space=pltpu.HBM)
SMEM = pl.BlockSpec(memory_space=pltpu.SMEM)
PARAMS = pltpu.CompilerParams(vmem_limit_bytes=10 * 1024 * 1024)
BF16 = jnp.bfloat16
F32 = jnp.float32


def hop(move):
    pairs = []
    for y in range(RING):
        for z in range(2):
            for c in range(2):
                y2, z2, c2 = move(y, z, c)
                pairs.append(((y * 2 + z) * 2 + c, ((y2 % RING) * 2 + z2) * 2 + c2))
    return pairs


CORE = hop(lambda y, z, c: (y, z, 1 - c))
ZSWAP = hop(lambda y, z, c: (y, 1 - z, c))


def ring(step):
    return hop(lambda y, z, c: (y + (1 - 2 * c) * step, z, c))


def send(value, pairs):
    return lax.ppermute(value, "fsdp", pairs)


def place():
    me = lax.axis_index("fsdp")
    return lax.rem(me, 2), lax.rem(lax.div(me, 2), 2), lax.div(me, 4)


def pick_kernel(away, x, *refs):
    core, zh, y = place()
    if away:
        k, out, sems = refs
        core = 1 - core
        copies = [pltpu.make_async_copy(k, out.at[:, pl.ds(2048, 512)], sems.at[16])]
    else:
        out, sems = refs
        copies = []
    for p, step in enumerate(ORDER):
        chunk = lax.rem(y + RING + (1 - 2 * core) * step, RING)
        for half in range(2):
            z = zh if half == 0 else 1 - zh
            start = pl.multiple_of((chunk * 4 + z * 2 + core) * 128, 128)
            j = 2 * p + half
            copies.append(
                pltpu.make_async_copy(
                    x.at[:, pl.ds(start, 128)], out.at[:, pl.ds(j * 128, 128)], sems.at[j]
                )
            )
    for copy in copies:
        copy.start()
    for copy in copies:
        copy.wait()


def pick(away, *operands):
    width = 2560 if away else 2048
    return pl.pallas_call(
        lambda *refs: pick_kernel(away, *refs),
        out_shape=jax.ShapeDtypeStruct((operands[0].shape[0], width), BF16),
        in_specs=[HBM] * len(operands),
        out_specs=ANY,
        scratch_shapes=[pltpu.SemaphoreType.DMA((17,))],
        compiler_params=PARAMS,
    )(*operands)


def call(kernel, shapes, specs, *operands, flops=0):
    return pl.pallas_call(
        kernel,
        out_shape=tuple(jax.ShapeDtypeStruct(shape, kind) for shape, kind in shapes),
        in_specs=specs,
        out_specs=(VMEM,) * len(shapes),
        compiler_params=PARAMS,
        cost_estimate=pl.CostEstimate(flops=flops, bytes_accessed=1 << 20, transcendentals=0),
    )(*operands)


def grad_kernel(scale, own, other, k, a, b, c4, d2, d6, d0):
    right = jnp.concatenate([k[...], other[:, 2048:2560]], axis=0)
    targets = ((a, 0), (a, 256), (b, 0), (b, 256), (c4, 0), (d2, 0), (d6, 0), (d0, 0))
    for p, (ref, row) in enumerate(targets):
        cols = slice(p * 256, p * 256 + 256)
        left = jnp.concatenate([own[:, cols], other[:, cols]], axis=0)
        part = scale * lax.dot_general(
            left, right, (((0,), (0,)), ((), ())), preferred_element_type=F32
        )
        ref[row : row + 256, :] = part.astype(ref.dtype)


def relay_kernel(d2, d6, a, b, c4, m2, m6):
    m2[...] = (d2[...] + a[256:, :].astype(F32) + c4[...].astype(F32)).astype(BF16)
    m6[...] = (d6[...] + b[256:, :].astype(F32)).astype(BF16)


def sum_of(d0, a, b, e2, e6, rows):
    near = a[rows, :].astype(F32) + b[rows, :].astype(F32)
    return d0[rows, :] + near + (e2[rows, :].astype(F32) + e6[rows, :].astype(F32))


def far_kernel(d0, a, b, e2, e6, out):
    out[...] = sum_of(d0, a, b, e2, e6, slice(128, 256)).astype(BF16)


def adam_kernel(d0, a, b, e2, e6, far, weight, anchor, first, second, mom, first_out, second_out, blocks):
    blocks[...] = jnp.zeros(blocks.shape, BF16)
    tiles, moms = [], []
    for r in range(8):
        rows = slice(16 * r, 16 * r + 16)
        grad = sum_of(d0, a, b, e2, e6, rows) + far[rows, :].astype(F32)
        first_new = 0.9 * first[0, rows, :] + 0.1 * grad
        second_new = 0.95 * second[0, rows, :] + 0.05 * grad * grad
        first_out[0, rows, :] = first_new
        second_out[0, rows, :] = second_new
        update = first_new / (1.0 - 0.9**8) / (jnp.sqrt(second_new / (1.0 - 0.95**8)) + 1e-08)
        w = weight[0, rows, :]
        delta = anchor[0, rows, :] - (w - 0.3 * (update + 0.1 * w))
        m = mom[0, rows, :]
        for s in range(2):
            for c in range(4):
                tiles.append(delta[8 * s : 8 * s + 8, 128 * c : 128 * c + 128])
                moms.append(m[8 * s : 8 * s + 8, 128 * c : 128 * c + 128])
        done = len(tiles) // 3 if r < 7 else -(-len(tiles) // 3)
        for j in range((len(tiles) - 8) // 3, done):
            group = tiles[3 * j : 3 * j + 3] + [None] * (3 - len(tiles[3 * j : 3 * j + 3]))
            group += moms[3 * j : 3 * j + 3] + [None] * (3 - len(moms[3 * j : 3 * j + 3]))
            group = [jnp.zeros((8, 128), F32) if t is None else t for t in group]
            for q in range(3):
                pair = jnp.concatenate([group[2 * q], group[2 * q + 1]], axis=0)
                blocks[j, 16 * q : 16 * q + 16, :] = pair.astype(BF16)


def mean_kernel(matching, got, mean):
    for r in range(got.shape[0]):
        mine = got[r].astype(F32)
        theirs = got[matching[0, r]].astype(F32)
        mean[r] = (0.5 * (mine + theirs)).astype(BF16)


def outer_kernel(back, anchor, anchor_out, mom_out):
    for j in range(-(-64 // 3)):
        group = []
        for q in range(3):
            pair = back[j, 16 * q : 16 * q + 16, :].astype(F32)
            group += [pair[:8], pair[8:]]
        for t in range(3):
            tile = 3 * j + t
            if tile < 64:
                rows = slice(tile // 4 * 8, tile // 4 * 8 + 8)
                cols = slice(tile % 4 * 128, tile % 4 * 128 + 128)
                delta_avg, mom_avg = group[t], group[3 + t]
                mom_new = 0.5 * mom_avg + delta_avg
                mom_out[0, rows, cols] = mom_new
                anchor_out[0, rows, cols] = anchor[0, rows, cols] - 0.7 * (
                    0.5 * mom_new + delta_avg
                )


def join_kernel(w0, w2, w6, left, right):
    left[:256, :] = w0[...]
    left[256:, :] = w6[...]
    right[:256, :] = w0[...]
    right[256:, :] = w2[...]


def key_kernel(scale, own, other, w0, w2, w6, from_left, from_right, w4, mine, theirs):
    near, far = slice(0, 256), slice(256, 512)
    blocks = (
        (from_right, near), (from_right, far), (from_left, near), (from_left, far),
        (w4, near), (w2, near), (w6, near), (w0, near),
    )
    total_mine = jnp.zeros(mine.shape, F32)
    total_theirs = jnp.zeros(theirs.shape, F32)
    for p, (ref, rows) in enumerate(blocks):
        cols = slice(p * 256, p * 256 + 256)
        block = ref[rows, :]
        total_theirs += jnp.dot(other[:, cols], block, preferred_element_type=F32)
        total_mine += jnp.dot(own[:, cols], block, preferred_element_type=F32)
    mine[...] = scale * total_mine
    theirs[...] = (scale * total_theirs).astype(theirs.dtype)


def on_device(inputs, key_grad, weights, anchor, adam_first, adam_second, outer_mom, partner):
    scale = inputs.shape[1] ** (-0.5)
    replicas = lax.axis_size("rep")
    tokens = inputs.shape[0]
    work = 4 * tokens * inputs.shape[1] * key_grad.shape[1] // 2

    in_place = pltpu.with_memory_space_constraint(inputs, pltpu.HBM)
    away = pick(True, in_place, pltpu.with_memory_space_constraint(key_grad, pltpu.HBM))
    other = send(away, CORE)
    own = pick(False, in_place)
    packed, own = lax.optimization_barrier((weights[0].astype(BF16), own))
    w0 = jnp.concatenate([packed, send(packed, ZSWAP)], axis=0)

    def piece(rows, kind=BF16):
        return ((rows, 512), kind)

    a, b, c4, d2, d6, d0 = call(
        lambda *refs: grad_kernel(scale, *refs),
        (piece(512), piece(512), piece(256), piece(256, F32), piece(256, F32), piece(256, F32)),
        [VMEM] * 3, own, other, key_grad, flops=work,
    )
    a, b, c4 = send(a, ring(1)), send(b, ring(-1)), send(c4, ring(2))
    m2, m6 = call(relay_kernel, (piece(256), piece(256)), [VMEM] * 5, d2, d6, a, b, c4)
    w0, m2, m6 = lax.optimization_barrier((w0, m2, m6))
    e2, e6 = send(m2, ring(2)), send(m6, ring(-2))
    (far,) = call(far_kernel, (piece(128),), [VMEM] * 5, d0, a, b, e2, e6)
    far = send(far, ZSWAP)
    w6, w2 = send(w0, ring(2)), send(w0, ring(-2))
    w2, far, w6 = lax.optimization_barrier((w2, far, w6))
    shard = (weights.shape, F32)
    block = -(-64 // replicas) * 16
    first_new, second_new, blocks = call(
        adam_kernel, (shard, shard, ((replicas, block, 128), BF16)), [VMEM] * 11,
        d0, a, b, e2, e6, far, weights, anchor, adam_first, adam_second, outer_mom,
    )
    blocks, w0 = lax.optimization_barrier((blocks, w0))
    got = lax.all_to_all(blocks, "rep", split_axis=0, concat_axis=0, tiled=True)
    left, right = call(join_kernel, (piece(512), piece(512)), [VMEM] * 3, w0, w2, w6)
    from_left, from_right, w4 = send(left, ring(1)), send(right, ring(-1)), send(w6, ring(2))
    (mean,) = call(mean_kernel, ((got.shape, BF16),), [SMEM, VMEM], partner, got)
    back = lax.all_to_all(mean, "rep", split_axis=0, concat_axis=0, tiled=True)
    mine, theirs = call(
        lambda *refs: key_kernel(scale, *refs),
        (((tokens, 512), F32), ((tokens, 512), BF16)),
        [VMEM] * 8, own, other, w0, w2, w6, from_left, from_right, w4, flops=work,
    )
    keys = (mine + send(theirs, CORE).astype(F32)).astype(BF16)
    anchor_new, mom_new = call(outer_kernel, (shard, shard), [VMEM] * 2, back, anchor)
    return (keys, anchor_new, mom_new, first_new, second_new)


def solution(mesh):
    shard = P("rep", "fsdp", None)
    flat = P(("rep", "fsdp"), None)
    return jax.shard_map(
        on_device,
        mesh=mesh,
        in_specs=(flat, flat, shard, shard, shard, shard, shard, P("fsdp", None)),
        out_specs=(flat, shard, shard, shard, shard),
        check_vma=False,
    )
```

```python
import jax
import jax.numpy as jnp
from jax import lax
from jax.experimental import pallas as pl
from jax.experimental.pallas import tpu as pltpu
from jax.sharding import PartitionSpec as P

RING = 8
ORDER = (1, 3, 7, 5, 4, 2, 6, 0)
VMEM = pl.BlockSpec(memory_space=pltpu.VMEM)
ANY = pl.BlockSpec(memory_space=pl.ANY)
HBM = pl.BlockSpec(memory_space=pltpu.HBM)
SMEM = pl.BlockSpec(memory_space=pltpu.SMEM)
PARAMS = pltpu.CompilerParams(vmem_limit_bytes=10 * 1024 * 1024)
BF16 = jnp.bfloat16
F32 = jnp.float32


def hop(move):
    pairs = []
    for y in range(RING):
        for z in range(2):
            for c in range(2):
                y2, z2, c2 = move(y, z, c)
                pairs.append(((y * 2 + z) * 2 + c, ((y2 % RING) * 2 + z2) * 2 + c2))
    return pairs


CORE = hop(lambda y, z, c: (y, z, 1 - c))
ZSWAP = hop(lambda y, z, c: (y, 1 - z, c))


def ring(step):
    return hop(lambda y, z, c: (y + (1 - 2 * c) * step, z, c))


def send(value, pairs):
    return lax.ppermute(value, "fsdp", pairs)


def place():
    me = lax.axis_index("fsdp")
    return lax.rem(me, 2), lax.rem(lax.div(me, 2), 2), lax.div(me, 4)


def pick_kernel(away, x, *refs):
    core, zh, y = place()
    if away:
        k, out, sems = refs
        core = 1 - core
        copies = [pltpu.make_async_copy(k, out.at[:, pl.ds(2048, 512)], sems.at[16])]
    else:
        out, sems = refs
        copies = []
    for p, step in enumerate(ORDER):
        chunk = lax.rem(y + RING + (1 - 2 * core) * step, RING)
        for half in range(2):
            z = zh if half == 0 else 1 - zh
            start = pl.multiple_of((chunk * 4 + z * 2 + core) * 128, 128)
            j = 2 * p + half
            copies.append(
                pltpu.make_async_copy(
                    x.at[:, pl.ds(start, 128)], out.at[:, pl.ds(j * 128, 128)], sems.at[j]
                )
            )
    for copy in copies:
        copy.start()
    for copy in copies:
        copy.wait()


def pick(away, *operands):
    width = 2560 if away else 2048
    return pl.pallas_call(
        lambda *refs: pick_kernel(away, *refs),
        out_shape=jax.ShapeDtypeStruct((operands[0].shape[0], width), BF16),
        in_specs=[HBM] * len(operands),
        out_specs=ANY,
        scratch_shapes=[pltpu.SemaphoreType.DMA((17,))],
        compiler_params=PARAMS,
    )(*operands)


def call(kernel, shapes, specs, *operands, flops=0):
    return pl.pallas_call(
        kernel,
        out_shape=tuple(jax.ShapeDtypeStruct(shape, kind) for shape, kind in shapes),
        in_specs=specs,
        out_specs=(VMEM,) * len(shapes),
        compiler_params=PARAMS,
        cost_estimate=pl.CostEstimate(flops=flops, bytes_accessed=1 << 20, transcendentals=0),
    )(*operands)


def grad_kernel(scale, own, other, k, a, b, c4, d2, d6, d0):
    right = jnp.concatenate([k[...], other[:, 2048:2560]], axis=0)
    targets = ((a, 0), (a, 256), (b, 0), (b, 256), (c4, 0), (d2, 0), (d6, 0), (d0, 0))
    for p, (ref, row) in enumerate(targets):
        cols = slice(p * 256, p * 256 + 256)
        left = jnp.concatenate([own[:, cols], other[:, cols]], axis=0)
        part = scale * lax.dot_general(
            left, right, (((0,), (0,)), ((), ())), preferred_element_type=F32
        )
        ref[row : row + 256, :] = part.astype(ref.dtype)


def relay_kernel(d2, d6, a, b, c4, m2, m6):
    m2[...] = (d2[...] + a[256:, :].astype(F32) + c4[...].astype(F32)).astype(BF16)
    m6[...] = (d6[...] + b[256:, :].astype(F32)).astype(BF16)


def sum_of(d0, a, b, e2, e6, rows):
    near = a[rows, :].astype(F32) + b[rows, :].astype(F32)
    return d0[rows, :] + near + (e2[rows, :].astype(F32) + e6[rows, :].astype(F32))


def far_kernel(d0, a, b, e2, e6, out):
    out[...] = sum_of(d0, a, b, e2, e6, slice(128, 256)).astype(BF16)


def adam_kernel(d0, a, b, e2, e6, far, weight, anchor, first, second, mom, first_out, second_out, blocks):
    blocks[...] = jnp.zeros(blocks.shape, BF16)
    tiles, moms = [], []
    for r in range(8):
        rows = slice(16 * r, 16 * r + 16)
        grad = sum_of(d0, a, b, e2, e6, rows) + far[rows, :].astype(F32)
        first_new = 0.9 * first[0, rows, :] + 0.1 * grad
        second_new = 0.95 * second[0, rows, :] + 0.05 * grad * grad
        first_out[0, rows, :] = first_new
        second_out[0, rows, :] = second_new
        update = first_new / (1.0 - 0.9**8) / (jnp.sqrt(second_new / (1.0 - 0.95**8)) + 1e-08)
        w = weight[0, rows, :]
        delta = anchor[0, rows, :] - (w - 0.3 * (update + 0.1 * w))
        m = mom[0, rows, :]
        for s in range(2):
            for c in range(4):
                tiles.append(delta[8 * s : 8 * s + 8, 128 * c : 128 * c + 128])
                moms.append(m[8 * s : 8 * s + 8, 128 * c : 128 * c + 128])
        done = len(tiles) // 3 if r < 7 else -(-len(tiles) // 3)
        for j in range((len(tiles) - 8) // 3, done):
            group = tiles[3 * j : 3 * j + 3] + [None] * (3 - len(tiles[3 * j : 3 * j + 3]))
            group += moms[3 * j : 3 * j + 3] + [None] * (3 - len(moms[3 * j : 3 * j + 3]))
            group = [jnp.zeros((8, 128), F32) if t is None else t for t in group]
            for q in range(3):
                pair = jnp.concatenate([group[2 * q], group[2 * q + 1]], axis=0)
                blocks[j, 16 * q : 16 * q + 16, :] = pair.astype(BF16)


def mean_kernel(matching, got, mean):
    for r in range(got.shape[0]):
        mine = got[r].astype(F32)
        theirs = got[matching[0, r]].astype(F32)
        mean[r] = (0.5 * (mine + theirs)).astype(BF16)


def outer_kernel(back, anchor, anchor_out, mom_out):
    for j in range(-(-64 // 3)):
        group = []
        for q in range(3):
            pair = back[j, 16 * q : 16 * q + 16, :].astype(F32)
            group += [pair[:8], pair[8:]]
        for t in range(3):
            tile = 3 * j + t
            if tile < 64:
                rows = slice(tile // 4 * 8, tile // 4 * 8 + 8)
                cols = slice(tile % 4 * 128, tile % 4 * 128 + 128)
                delta_avg, mom_avg = group[t], group[3 + t]
                mom_new = 0.5 * mom_avg + delta_avg
                mom_out[0, rows, cols] = mom_new
                anchor_out[0, rows, cols] = anchor[0, rows, cols] - 0.7 * (
                    0.5 * mom_new + delta_avg
                )


def join_kernel(w0, w2, w6, left, right):
    left[:256, :] = w0[...]
    left[256:, :] = w6[...]
    right[:256, :] = w0[...]
    right[256:, :] = w2[...]


def key_kernel(own, other, w0, w2, w6, from_left, from_right, mine, theirs):
    near, far = slice(0, 256), slice(256, 512)
    blocks = (
        (from_right, near), (from_right, far), (from_left, near), (from_left, far),
        None, (w2, near), (w6, near), (w0, near),
    )
    total_mine = jnp.zeros(mine.shape, F32)
    total_theirs = jnp.zeros(theirs.shape, F32)
    for p, place in enumerate(blocks):
        if place is not None:
            cols = slice(p * 256, p * 256 + 256)
            block = place[0][place[1], :]
            total_theirs += jnp.dot(other[:, cols], block, preferred_element_type=F32)
            total_mine += jnp.dot(own[:, cols], block, preferred_element_type=F32)
    mine[...] = total_mine
    theirs[...] = total_theirs


def last_key_kernel(scale, own, other, w4, mine_in, theirs_in, mine, theirs):
    cols = slice(1024, 1280)
    block = w4[...]
    part = theirs_in[...] + jnp.dot(other[:, cols], block, preferred_element_type=F32)
    theirs[...] = (scale * part).astype(theirs.dtype)
    part = mine_in[...] + jnp.dot(own[:, cols], block, preferred_element_type=F32)
    mine[...] = scale * part


def on_device(inputs, key_grad, weights, anchor, adam_first, adam_second, outer_mom, partner):
    scale = inputs.shape[1] ** (-0.5)
    replicas = lax.axis_size("rep")
    tokens = inputs.shape[0]
    work = 4 * tokens * inputs.shape[1] * key_grad.shape[1] // 2

    in_place = pltpu.with_memory_space_constraint(inputs, pltpu.HBM)
    away = pick(True, in_place, pltpu.with_memory_space_constraint(key_grad, pltpu.HBM))
    other = send(away, CORE)
    own = pick(False, in_place)
    packed, own = lax.optimization_barrier((weights[0].astype(BF16), own))
    w0 = jnp.concatenate([packed, send(packed, ZSWAP)], axis=0)

    def piece(rows, kind=BF16):
        return ((rows, 512), kind)

    a, b, c4, d2, d6, d0 = call(
        lambda *refs: grad_kernel(scale, *refs),
        (piece(512), piece(512), piece(256), piece(256, F32), piece(256, F32), piece(256, F32)),
        [VMEM] * 3, own, other, key_grad, flops=work,
    )
    a, b, c4 = send(a, ring(1)), send(b, ring(-1)), send(c4, ring(2))
    m2, m6 = call(relay_kernel, (piece(256), piece(256)), [VMEM] * 5, d2, d6, a, b, c4)
    e2, e6 = send(m2, ring(2)), send(m6, ring(-2))
    (far,) = call(far_kernel, (piece(128),), [VMEM] * 5, d0, a, b, e2, e6)
    far = send(far, ZSWAP)
    w6, w2 = send(w0, ring(2)), send(w0, ring(-2))
    w2, far, w6 = lax.optimization_barrier((w2, far, w6))
    shard = (weights.shape, F32)
    block = -(-64 // replicas) * 16
    first_new, second_new, blocks = call(
        adam_kernel, (shard, shard, ((replicas, block, 128), BF16)), [VMEM] * 11,
        d0, a, b, e2, e6, far, weights, anchor, adam_first, adam_second, outer_mom,
    )
    blocks, w0 = lax.optimization_barrier((blocks, w0))
    got = lax.all_to_all(blocks, "rep", split_axis=0, concat_axis=0, tiled=True)
    left, right = call(join_kernel, (piece(512), piece(512)), [VMEM] * 3, w0, w2, w6)
    from_left, from_right, w4 = send(left, ring(1)), send(right, ring(-1)), send(w6, ring(2))
    (mean,) = call(mean_kernel, ((got.shape, BF16),), [SMEM, VMEM], partner, got)
    back = lax.all_to_all(mean, "rep", split_axis=0, concat_axis=0, tiled=True)
    partial = ((tokens, 512), F32)
    mine, theirs = call(
        key_kernel, (partial, partial),
        [VMEM] * 7, own, other, w0, w2, w6, from_left, from_right, flops=work,
    )
    mine, theirs = call(
        lambda *refs: last_key_kernel(scale, *refs), (partial, ((tokens, 512), BF16)),
        [VMEM] * 5, own, other, w4, mine, theirs, flops=work // 8,
    )
    keys = (mine + send(theirs, CORE).astype(F32)).astype(BF16)
    anchor_new, mom_new = call(outer_kernel, (shard, shard), [VMEM] * 2, back, anchor)
    return (keys, anchor_new, mom_new, first_new, second_new)


def solution(mesh):
    shard = P("rep", "fsdp", None)
    flat = P(("rep", "fsdp"), None)
    return jax.shard_map(
        on_device,
        mesh=mesh,
        in_specs=(flat, flat, shard, shard, shard, shard, shard, P("fsdp", None)),
        out_specs=(flat, shard, shard, shard, shard),
        check_vma=False,
    )
```

```python
import jax
import jax.numpy as jnp
from jax import lax
from jax.experimental import pallas as pl
from jax.experimental.pallas import tpu as pltpu
from jax.sharding import PartitionSpec as P

RING = 8
ORDER = (1, 3, 7, 5, 4, 2, 6, 0)
VMEM = pl.BlockSpec(memory_space=pltpu.VMEM)
ANY = pl.BlockSpec(memory_space=pl.ANY)
HBM = pl.BlockSpec(memory_space=pltpu.HBM)
SMEM = pl.BlockSpec(memory_space=pltpu.SMEM)
PARAMS = pltpu.CompilerParams(vmem_limit_bytes=10 * 1024 * 1024)
BF16 = jnp.bfloat16
F32 = jnp.float32


def hop(move):
    pairs = []
    for y in range(RING):
        for z in range(2):
            for c in range(2):
                y2, z2, c2 = move(y, z, c)
                pairs.append(((y * 2 + z) * 2 + c, ((y2 % RING) * 2 + z2) * 2 + c2))
    return pairs


CORE = hop(lambda y, z, c: (y, z, 1 - c))
ZSWAP = hop(lambda y, z, c: (y, 1 - z, c))


def ring(step):
    return hop(lambda y, z, c: (y + (1 - 2 * c) * step, z, c))


def send(value, pairs):
    return lax.ppermute(value, "fsdp", pairs)


def place():
    me = lax.axis_index("fsdp")
    return lax.rem(me, 2), lax.rem(lax.div(me, 2), 2), lax.div(me, 4)


def pick_kernel(away, x, *refs):
    core, zh, y = place()
    if away:
        k, out, sems = refs
        core = 1 - core
        copies = [pltpu.make_async_copy(k, out.at[:, pl.ds(2048, 512)], sems.at[16])]
    else:
        out, sems = refs
        copies = []
    for p, step in enumerate(ORDER):
        chunk = lax.rem(y + RING + (1 - 2 * core) * step, RING)
        for half in range(2):
            z = zh if half == 0 else 1 - zh
            start = pl.multiple_of((chunk * 4 + z * 2 + core) * 128, 128)
            j = 2 * p + half
            copies.append(
                pltpu.make_async_copy(
                    x.at[:, pl.ds(start, 128)], out.at[:, pl.ds(j * 128, 128)], sems.at[j]
                )
            )
    for copy in copies:
        copy.start()
    for copy in copies:
        copy.wait()


def pick(away, *operands):
    width = 2560 if away else 2048
    return pl.pallas_call(
        lambda *refs: pick_kernel(away, *refs),
        out_shape=jax.ShapeDtypeStruct((operands[0].shape[0], width), BF16),
        in_specs=[HBM] * len(operands),
        out_specs=ANY,
        scratch_shapes=[pltpu.SemaphoreType.DMA((17,))],
        compiler_params=PARAMS,
    )(*operands)


def call(kernel, shapes, specs, *operands, flops=0):
    return pl.pallas_call(
        kernel,
        out_shape=tuple(jax.ShapeDtypeStruct(shape, kind) for shape, kind in shapes),
        in_specs=specs,
        out_specs=(VMEM,) * len(shapes),
        compiler_params=PARAMS,
        cost_estimate=pl.CostEstimate(flops=flops, bytes_accessed=1 << 20, transcendentals=0),
    )(*operands)


def grad_kernel(scale, own, other, k, a, b, c4, d2, d6, d0):
    right = jnp.concatenate([k[...], other[:, 2048:2560]], axis=0)
    targets = ((a, 0), (a, 256), (b, 0), (b, 256), (c4, 0), (d2, 0), (d6, 0), (d0, 0))
    for p, (ref, row) in enumerate(targets):
        cols = slice(p * 256, p * 256 + 256)
        left = jnp.concatenate([own[:, cols], other[:, cols]], axis=0)
        part = scale * lax.dot_general(
            left, right, (((0,), (0,)), ((), ())), preferred_element_type=F32
        )
        ref[row : row + 256, :] = part.astype(ref.dtype)


def relay_kernel(d2, d6, a, b, c4, m2, m6):
    m2[...] = (d2[...] + a[256:, :].astype(F32) + c4[...].astype(F32)).astype(BF16)
    m6[...] = (d6[...] + b[256:, :].astype(F32)).astype(BF16)


def sum_of(d0, a, b, e2, e6, rows):
    near = a[rows, :].astype(F32) + b[rows, :].astype(F32)
    return d0[rows, :] + near + (e2[rows, :].astype(F32) + e6[rows, :].astype(F32))


def far_kernel(d0, a, b, e2, e6, out):
    out[...] = sum_of(d0, a, b, e2, e6, slice(128, 256)).astype(BF16)


def adam_kernel(d0, a, b, e2, e6, far, weight, anchor, first, second, mom, first_out, second_out, blocks):
    blocks[...] = jnp.zeros(blocks.shape, BF16)
    tiles, moms = [], []
    for r in range(8):
        rows = slice(16 * r, 16 * r + 16)
        grad = sum_of(d0, a, b, e2, e6, rows) + far[rows, :].astype(F32)
        first_new = 0.9 * first[0, rows, :] + 0.1 * grad
        second_new = 0.95 * second[0, rows, :] + 0.05 * grad * grad
        first_out[0, rows, :] = first_new
        second_out[0, rows, :] = second_new
        update = first_new / (1.0 - 0.9**8) / (jnp.sqrt(second_new / (1.0 - 0.95**8)) + 1e-08)
        w = weight[0, rows, :]
        delta = anchor[0, rows, :] - (w - 0.3 * (update + 0.1 * w))
        m = mom[0, rows, :]
        for s in range(2):
            for c in range(4):
                tiles.append(delta[8 * s : 8 * s + 8, 128 * c : 128 * c + 128])
                moms.append(m[8 * s : 8 * s + 8, 128 * c : 128 * c + 128])
        done = len(tiles) // 3 if r < 7 else -(-len(tiles) // 3)
        for j in range((len(tiles) - 8) // 3, done):
            group = tiles[3 * j : 3 * j + 3] + [None] * (3 - len(tiles[3 * j : 3 * j + 3]))
            group += moms[3 * j : 3 * j + 3] + [None] * (3 - len(moms[3 * j : 3 * j + 3]))
            group = [jnp.zeros((8, 128), F32) if t is None else t for t in group]
            for q in range(3):
                pair = jnp.concatenate([group[2 * q], group[2 * q + 1]], axis=0)
                blocks[j, 16 * q : 16 * q + 16, :] = pair.astype(BF16)


def mean_kernel(matching, got, mean):
    for r in range(got.shape[0]):
        mine = got[r].astype(F32)
        theirs = got[matching[0, r]].astype(F32)
        mean[r] = (0.5 * (mine + theirs)).astype(BF16)


def outer_kernel(back, anchor, anchor_out, mom_out):
    for j in range(-(-64 // 3)):
        group = []
        for q in range(3):
            pair = back[j, 16 * q : 16 * q + 16, :].astype(F32)
            group += [pair[:8], pair[8:]]
        for t in range(3):
            tile = 3 * j + t
            if tile < 64:
                rows = slice(tile // 4 * 8, tile // 4 * 8 + 8)
                cols = slice(tile % 4 * 128, tile % 4 * 128 + 128)
                delta_avg, mom_avg = group[t], group[3 + t]
                mom_new = 0.5 * mom_avg + delta_avg
                mom_out[0, rows, cols] = mom_new
                anchor_out[0, rows, cols] = anchor[0, rows, cols] - 0.7 * (
                    0.5 * mom_new + delta_avg
                )


def join_kernel(w0, w2, w6, left, right):
    left[:256, :] = w0[...]
    left[256:, :] = w6[...]
    right[:256, :] = w0[...]
    right[256:, :] = w2[...]


def key_kernel(own, other, w0, w2, w6, from_left, from_right, mine, theirs):
    near, far = slice(0, 256), slice(256, 512)
    blocks = (
        (from_right, near), (from_right, far), (from_left, near), (from_left, far),
        None, (w2, near), (w6, near), (w0, near),
    )
    total_mine = jnp.zeros(mine.shape, F32)
    total_theirs = jnp.zeros(theirs.shape, F32)
    for p, place in enumerate(blocks):
        if place is not None:
            cols = slice(p * 256, p * 256 + 256)
            block = place[0][place[1], :]
            total_theirs += jnp.dot(other[:, cols], block, preferred_element_type=F32)
            total_mine += jnp.dot(own[:, cols], block, preferred_element_type=F32)
    mine[...] = total_mine
    theirs[...] = total_theirs


def last_key_kernel(scale, own, other, w4, mine_in, theirs_in, mine, theirs):
    cols = slice(1024, 1280)
    block = w4[...]
    part = theirs_in[...] + jnp.dot(other[:, cols], block, preferred_element_type=F32)
    theirs[...] = (scale * part).astype(theirs.dtype)
    part = mine_in[...] + jnp.dot(own[:, cols], block, preferred_element_type=F32)
    mine[...] = scale * part


def on_device(inputs, key_grad, weights, anchor, adam_first, adam_second, outer_mom, partner):
    scale = inputs.shape[1] ** (-0.5)
    replicas = lax.axis_size("rep")
    tokens = inputs.shape[0]
    work = 4 * tokens * inputs.shape[1] * key_grad.shape[1] // 2

    in_place = pltpu.with_memory_space_constraint(inputs, pltpu.HBM)
    away = pick(True, in_place, pltpu.with_memory_space_constraint(key_grad, pltpu.HBM))
    other = send(away, CORE)
    own = pick(False, in_place)
    packed, own = lax.optimization_barrier((weights[0].astype(BF16), own))
    w0 = jnp.concatenate([packed, send(packed, ZSWAP)], axis=0)

    def piece(rows, kind=BF16):
        return ((rows, 512), kind)

    a, b, c4, d2, d6, d0 = call(
        lambda *refs: grad_kernel(scale, *refs),
        (piece(512), piece(512), piece(256), piece(256, F32), piece(256, F32), piece(256, F32)),
        [VMEM] * 3, own, other, key_grad, flops=work,
    )
    a, b, c4 = send(a, ring(1)), send(b, ring(-1)), send(c4, ring(2))
    m2, m6 = call(relay_kernel, (piece(256), piece(256)), [VMEM] * 5, d2, d6, a, b, c4)
    e2, e6 = send(m2, ring(2)), send(m6, ring(-2))
    (far,) = call(far_kernel, (piece(128),), [VMEM] * 5, d0, a, b, e2, e6)
    far = send(far, ZSWAP)
    w6, w2 = send(w0, ring(2)), send(w0, ring(-2))
    left, right = call(join_kernel, (piece(512), piece(512)), [VMEM] * 3, w0, w2, w6)
    left, far, right, w6 = lax.optimization_barrier((left, far, right, w6))
    shard = (weights.shape, F32)
    block = -(-64 // replicas) * 16
    first_new, second_new, blocks = call(
        adam_kernel, (shard, shard, ((replicas, block, 128), BF16)), [VMEM] * 11,
        d0, a, b, e2, e6, far, weights, anchor, adam_first, adam_second, outer_mom,
    )
    blocks, w0 = lax.optimization_barrier((blocks, w0))
    got = lax.all_to_all(blocks, "rep", split_axis=0, concat_axis=0, tiled=True)
    from_left, from_right, w4 = send(left, ring(1)), send(right, ring(-1)), send(w6, ring(2))
    (mean,) = call(mean_kernel, ((got.shape, BF16),), [SMEM, VMEM], partner, got)
    w4, mean = lax.optimization_barrier((w4, mean))
    back = lax.all_to_all(mean, "rep", split_axis=0, concat_axis=0, tiled=True)
    partial = ((tokens, 512), F32)
    mine, theirs = call(
        key_kernel, (partial, partial),
        [VMEM] * 7, own, other, w0, w2, w6, from_left, from_right, flops=work,
    )
    mine, theirs = call(
        lambda *refs: last_key_kernel(scale, *refs), (partial, ((tokens, 512), BF16)),
        [VMEM] * 5, own, other, w4, mine, theirs, flops=work // 8,
    )
    keys = (mine + send(theirs, CORE).astype(F32)).astype(BF16)
    anchor_new, mom_new = call(outer_kernel, (shard, shard), [VMEM] * 2, back, anchor)
    return (keys, anchor_new, mom_new, first_new, second_new)


def solution(mesh):
    shard = P("rep", "fsdp", None)
    flat = P(("rep", "fsdp"), None)
    return jax.shard_map(
        on_device,
        mesh=mesh,
        in_specs=(flat, flat, shard, shard, shard, shard, shard, P("fsdp", None)),
        out_specs=(flat, shard, shard, shard, shard),
        check_vma=False,
    )
```
